32 devices in a mesh: gx: 4 (over x, core), gy: 8 (over z, y).
Axes of the slice: x: 2, y: 2, z: 4, core: 2. Of those that a mesh axis runs over, the one named last changes fastest.
Arguments:
- fields: float32 [8192, 2, 1024], P(('gx', 'gy')), may hold values from -6 to 6
- aperture: float32 [8192, 1024], P(('gx', 'gy')), may hold values from 0.1 to 1
- source: float32 [8192, 2, 1024], P(('gx', 'gy')), may hold values from -6 to 6
- storage: float32 [8192, 2], P(('gx', 'gy')), may hold values from 0.02 to 0.5
- coarse_weight: float32 [25088], replicated, may hold values from 0.3 to 3
- source_slot: int32 [131072], P(('gx', 'gy')), may hold values from 0 to 255
- source_edge: int32 [131072], P(('gx', 'gy')), may hold values from 0 to 3
- destination: int32 [131072, 1], P(('gx', 'gy')), may hold values from 0 to 31; in each aligned block of 4096 rows (0 to 4095, 4096 to 8191, ...) at most 128 rows name the same one
- target_frac: int32 [131072], P(('gx', 'gy')), may hold values from 0 to 255
- target_edge: int32 [131072], P(('gx', 'gy')), may hold values from 0 to 3
- coarse_index: int32 [131072], P(('gx', 'gy')), may hold values from 0 to 25087, as said below
Outputs:
- fields_out: float32 [8192, 2, 1024], P(('gx', 'gy'))
- coarse_out: float32 [25088], replicated
The draws below stay inside these ranges and needn't reach their ends.
Inputs may be any that keep to these rules, and one draw needn't show every extreme that they name: In the records of one device no destination occurs more than 128 times, and some destination occurs exactly 128 times. `coarse_index`: A record of device d names a coarse unknown of d * 784 to (d + 1) * 784 - 1.
All inputs are finite; a program needn't handle non-finite values.
Results may differ from the reference program's by a relative error of at most 0.0001.
Values sent between devices are 32-bit elements; how exact they have to be, the bound alone decides.
A program may use at most 128 MiB of HBM per device.

```python
import math
import jax
import jax.numpy as jnp
import numpy as np

GRID = 32
FR_DEV = 256
INT_DEV = 4096
COARSE_DEV = 784
ITERS = 2
SWEEPS = 8
SLOT = 128
FRACS = 8192
INTER = 131072
COARSE = 25088
DEVICES = 32


def draw_coarse_index(key, part):
    key = jax.random.fold_in(key, 7)
    local = jax.random.randint(key, (INTER,), 0, COARSE_DEV)
    owner = jnp.arange(INTER) // INT_DEV
    return (owner * COARSE_DEV + local).astype(jnp.int32)


def set_ends(entries, rng, low, largest):
    extent = entries.shape
    index_at = [jax.random.randint(jax.random.fold_in(rng, axis), (), 0, extent[axis]) for axis in range(len(extent))]
    entries = entries.at[tuple(index_at)].set(low)
    longest = extent.index(max(extent))
    index_at[longest] = (index_at[longest] + 1) % extent[longest]
    return entries.at[tuple(index_at)].set(largest)


def block_levels(own_key, extent, shards, least, high):
    factor_of, own = 1.0, jax.random.fold_in(own_key, 6)
    for position, blocks in shards:
        draws = jnp.exp(jax.random.uniform(jax.random.fold_in(own, position), (blocks,), jnp.float32, least / len(shards), high / len(shards)))
        factor_of = factor_of * jnp.repeat(draws, extent[position] // blocks).reshape([-1 if axis == position else 1 for axis in range(len(extent))])
    return factor_of


def shared_out(stream_key, own, number, rows, count, top, bound, skew):
    sequence = jax.random.permutation(stream_key, count)
    packed, usual = load_shares(count, rows * top, bound, skew, True), load_shares(count, rows * top, bound, skew, False)
    places = jnp.arange(count)

    def named(sizes, offset_by):
        used = int((sizes > 0).sum())
        fixed = max(1, used // 4)
        shifted = fixed + (places - fixed + offset_by * (used - fixed)) % max(1, count - fixed)
        return jnp.zeros((count,), jnp.int32).at[sequence[jnp.where(places < fixed, places, shifted)]].set(jnp.asarray(sizes, jnp.int32))

    sizes = jnp.where(number % 4 == 0, named(packed, number // 4), named(usual, number - number // 4 - 1))
    mixed = jax.random.permutation(jax.random.fold_in(own, 3), count)
    giver, taker = mixed[0:count // 2 * 2:2], mixed[1:count // 2 * 2:2]
    room = jnp.minimum(sizes[giver] - 1, bound - sizes[taker]) // 2
    room = jnp.where((giver == sequence[0]) | (taker == sequence[0]) | (sizes[taker] == 0), 0, jnp.maximum(room, 0))
    shifted = jax.random.randint(jax.random.fold_in(own, 4), (count // 2,), 0, 1 << 20) % (room + 1)
    sizes = sizes.at[giver].add(-shifted).at[taker].add(shifted)
    items = jnp.searchsorted(jnp.cumsum(sizes), jnp.arange(rows * top), side="right").astype(jnp.int32)
    table = items.reshape(top, rows).T
    table = table[jax.random.permutation(jax.random.fold_in(own, 1), rows)]
    offset_by = jax.random.randint(jax.random.fold_in(own, 2), (rows, 1), 0, top)
    return jnp.take_along_axis(table, (jnp.arange(top)[None, :] + offset_by) % top, axis=1)


def load_shares(number_of, total, most, skew, full):
    loads = [(1 << 20) // math.isqrt(rank ** skew) + 1 for rank in range(1, number_of + 1)]
    largest = most if full else min(most, max(-(-total // number_of), total * loads[0] // sum(loads)))
    least = 1 if total - largest >= number_of - 1 else 0
    given, rest = [largest] + [least] * (number_of - 1), total - largest - least * (number_of - 1)
    while rest > 0:
        candidates = [i for i in range(1, number_of) if given[i] < largest] or [i for i in range(1, number_of) if given[i] < most]
        whole, budget = sum([loads[i] for i in candidates]), rest
        for i in candidates:
            addition = min(most - given[i], max(1, budget * loads[i] // whole), rest)
            given[i] = given[i] + addition
            rest = rest - addition
    return np.array(given)


def scatter_about(own_key, extent, spread, bound, cuts=(), held_as=jnp.bfloat16):
    gain = block_levels(own_key, extent, cuts, -0.22, 0.18) if cuts else 1.0
    array = jax.random.normal(own_key, extent, jnp.float32) * spread * gain
    return jnp.minimum(jnp.maximum(array, -bound), bound).astype(held_as)


def setup_inputs(seed: int = 0) -> dict:
    key_of = jax.random.split(jax.random.key(seed), 12)
    fields = scatter_about(key_of[0], (FRACS, 2, GRID * GRID), 1.0, 6.0, ((0, 32),), jnp.float32)
    aperture = jnp.clip(jnp.exp(math.log(1.0) - 2.3025851 * jax.random.uniform(key_of[1], (FRACS, GRID * GRID), jnp.float32) ** block_levels(key_of[1], (FRACS, GRID * GRID), ((0, 32),), -0.2, 0.2)), 0.1, 1.0)
    source = scatter_about(key_of[2], (FRACS, 2, GRID * GRID), 1.0, 6.0, ((0, 32),), jnp.float32)
    storage = jnp.clip(jnp.exp(math.log(0.5) - 3.218876 * jax.random.uniform(key_of[3], (FRACS, 2), jnp.float32) ** block_levels(key_of[3], (FRACS, 2), ((0, 32),), -0.2, 0.2)), 0.02, 0.5)
    coarse_weight = jnp.clip(jnp.exp(jax.random.uniform(key_of[4], (COARSE,), jnp.float32, math.log(0.3), math.log(3.0))), 0.3, 3.0)
    source_slot = set_ends(jax.random.randint(key_of[5], (INTER,), 0, FR_DEV), jax.random.fold_in(key_of[5], 1), 0, FR_DEV - 1).astype(jnp.int32)
    source_edge = set_ends(jax.random.randint(key_of[6], (INTER,), 0, 4), jax.random.fold_in(key_of[6], 1), 0, 3).astype(jnp.int32)
    destination_keys = jax.random.split(jax.random.fold_in(key_of[7], 1), INTER // INT_DEV)
    destination_turns = jax.random.permutation(jax.random.fold_in(key_of[7], 3), INTER // INT_DEV)
    destination = jax.vmap(lambda own, number: shared_out(jax.random.fold_in(key_of[7], 2), own, number, INT_DEV, DEVICES, 1, SLOT, 2))(destination_keys, destination_turns).reshape((INTER, 1))
    target_frac = set_ends(jax.random.randint(key_of[8], (INTER,), 0, FR_DEV), jax.random.fold_in(key_of[8], 1), 0, FR_DEV - 1).astype(jnp.int32)
    target_edge = set_ends(jax.random.randint(key_of[9], (INTER,), 0, 4), jax.random.fold_in(key_of[9], 1), 0, 3).astype(jnp.int32)
    coarse_index = draw_coarse_index(jax.random.fold_in(key_of[11], 71), 0)
    return dict(fields=fields, aperture=aperture, source=source, storage=storage, coarse_weight=coarse_weight, source_slot=source_slot, source_edge=source_edge, destination=destination, target_frac=target_frac, target_edge=target_edge, coarse_index=coarse_index)


def edge_rows(fields):
    cells = GRID * GRID
    top = fields[:, :, :GRID]
    bottom = fields[:, :, cells - GRID:]
    left = fields[:, :, 0::GRID]
    right = fields[:, :, GRID - 1::GRID]
    return jnp.stack([top, bottom, left, right], 1)


def face_terms(aperture, storage):
    column = jnp.arange(GRID * GRID) % GRID
    a_up = jnp.concatenate([aperture[:, :GRID], aperture[:, :-GRID]], 1)
    a_down = jnp.concatenate([aperture[:, GRID:], aperture[:, -GRID:]], 1)
    a_left = jnp.where(column == 0, aperture, jnp.concatenate([aperture[:, :1], aperture[:, :-1]], 1))
    a_right = jnp.where(column == GRID - 1, aperture, jnp.concatenate([aperture[:, 1:], aperture[:, -1:]], 1))
    w_up = (0.5 * (aperture + a_up))[:, None, :]
    w_down = (0.5 * (aperture + a_down))[:, None, :]
    w_left = (0.5 * (aperture + a_left))[:, None, :]
    w_right = (0.5 * (aperture + a_right))[:, None, :]
    diag = storage[:, :, None] + w_up + w_down + w_left + w_right
    return w_up, w_down, w_left, w_right, diag


def sweeps(fields, boundary, faces, source):
    w_up, w_down, w_left, w_right, diag = faces
    column = jnp.arange(GRID * GRID) % GRID
    top = boundary[:, 0]
    bottom = boundary[:, 1]
    left = jnp.repeat(boundary[:, 2], GRID, axis=-1)
    right = jnp.repeat(boundary[:, 3], GRID, axis=-1)
    for sweep in range(SWEEPS):
        upper = jnp.concatenate([top, fields[:, :, :-GRID]], -1)
        lower = jnp.concatenate([fields[:, :, GRID:], bottom], -1)
        west = jnp.where(column == 0, left, jnp.concatenate([fields[:, :, :1], fields[:, :, :-1]], -1))
        east = jnp.where(column == GRID - 1, right, jnp.concatenate([fields[:, :, 1:], fields[:, :, -1:]], -1))
        fields = (source + w_up * upper + w_down * lower + w_left * west + w_right * east) / diag
    return fields


def reference(fields, aperture, source, storage, coarse_weight, source_slot, source_edge, destination, target_frac, target_edge, coarse_index):
    fracs = fields.shape[0]
    inter = source_slot.shape[0]
    owner = (jnp.arange(inter) // INT_DEV).astype(jnp.int32)
    sender = (owner * FR_DEV + source_slot) * 4 + source_edge
    receiver = (destination[:, 0] * FR_DEV + target_frac) * 4 + target_edge
    faces = face_terms(aperture, storage)
    counts = jax.ops.segment_sum(jnp.ones((inter,), jnp.float32), receiver, fracs * 4)
    correction = jnp.zeros((COARSE,), jnp.float32)
    for step in range(ITERS):
        edges = edge_rows(fields).reshape(fracs * 4, 2 * GRID)
        rows = edges[sender]
        own = edges[receiver]
        mismatch = jnp.mean(rows[:, :GRID] - own[:, :GRID], axis=1)
        correction = coarse_weight * jax.ops.segment_sum(mismatch, coarse_index, COARSE)
        values = rows + correction[coarse_index][:, None]
        incoming = jax.ops.segment_sum(values, receiver, fracs * 4)
        boundary = ((edges + incoming) / (1.0 + counts)[:, None]).reshape(fracs, 4, 2, GRID)
        fields = sweeps(fields, boundary, faces, source)
    return fields, correction
```

```python
import functools

import jax
import jax.numpy as jnp
from jax import lax
from jax.experimental import pallas as pl
from jax.experimental.pallas import tpu as pltpu
from jax.sharding import PartitionSpec as P

GRID = 32
ITERS = 2
SWEEPS = 8
SLOT = 128
LANES = 128
TILES = GRID * GRID // LANES
AXES = ("gx", "gy")
NT = (((1,), (1,)), ((), ()))
NN = (((1,), (0,)), ((), ()))


def dot(a, b, dims):
    return lax.dot_general(a, b, dims, preferred_element_type=jnp.float32)


def dot_exact(a, b, dims):
    return lax.dot_general(
        a, b, dims, precision=lax.Precision.HIGHEST, preferred_element_type=jnp.float32
    )


def split3(x):
    high = x.astype(jnp.bfloat16)
    rest = x - high.astype(jnp.float32)
    mid = rest.astype(jnp.bfloat16)
    low = (rest - mid.astype(jnp.float32)).astype(jnp.bfloat16)
    return high, mid, low


def iota(shape, dim):
    return lax.broadcasted_iota(jnp.int32, shape, dim)


def equal(a, b, dtype=jnp.bfloat16):
    return jnp.where(a == b, 1.0, 0.0).astype(dtype)


def slots_body(peers, fracs, record_ref, sender_ref, target_ref, coarse_ref):
    chunk = 512
    count = record_ref.shape[1]
    upto = (iota((chunk, chunk), 0) <= iota((chunk, chunk), 1)).astype(jnp.float32)
    upto = upto.astype(jnp.bfloat16)
    base = jnp.zeros((peers, 1), jnp.float32)
    total = jnp.zeros((6 * peers, SLOT), jnp.float32)
    for start in range(0, count, chunk):
        rows = [record_ref[i : i + 1, start : start + chunk] for i in range(7)]
        onehot = equal(iota((peers, chunk), 0), rows[0], jnp.float32)
        running = dot(onehot.astype(jnp.bfloat16), upto, NN)
        place = jnp.sum(onehot * (running + base), 0, keepdims=True) - 1.0
        base = base + running[:, chunk - 1 :]
        at_place = equal(iota((SLOT, chunk), 0), place.astype(jnp.int32))
        parts = [onehot * rows[i].astype(jnp.float32) for i in range(1, 7)]
        total = total + dot(jnp.concatenate(parts, 0).astype(jnp.bfloat16), at_place, NT)
    table = (total + 0.5).astype(jnp.int32)
    pieces = [table[i * peers : (i + 1) * peers] for i in range(6)]
    valid = pieces[3] > 0
    sender_ref[...] = jnp.where(valid, pieces[1] * fracs + pieces[0], -1)
    target_ref[...] = jnp.where(valid, (pieces[3] - 1) * fracs + pieces[2], -1)
    coarse_ref[...] = jnp.where(valid, pieces[4] * LANES + pieces[5], -1)


def edge_selector(tile):
    row = iota((4 * GRID, LANES), 0)
    k, edge = row & (GRID - 1), row >> 5
    cell = jnp.where(
        edge == 0,
        k,
        jnp.where(edge == 1, GRID * (GRID - 1) + k, k * GRID + (edge - 2) * (GRID - 1)),
    )
    return (iota((4 * GRID, LANES), 1) + tile * LANES) == cell


def edge_and_frac(code, fracs):
    shift = fracs.bit_length() - 1
    return jnp.where(code >= 0, code >> shift, -1), jnp.where(code >= 0, code & (fracs - 1), -1)


def edges_body(peers, fracs, fields_ref, sender_ref, edges_ref, rows_ref, mean_ref, split_ref):
    for c in range(2):
        total = jnp.zeros((4 * GRID, fracs), jnp.float32)
        for tile in range(TILES):
            cells = fields_ref[pl.ds(tile * 2 + c, fracs, stride=2 * TILES), :]
            selector = edge_selector(tile).astype(jnp.float32).astype(jnp.bfloat16)
            for part in split3(cells):
                total = total + dot(selector, part, NT)
        edges_ref[c * 4 * GRID : (c + 1) * 4 * GRID, :] = total
        for i, part in enumerate(split3(total)):
            start = i * 8 * GRID + c * 4 * GRID
            split_ref[start : start + 4 * GRID, :] = part

    def one_peer(d, carry):
        edge, frac = edge_and_frac(sender_ref[pl.ds(d, 1), :], fracs)
        onehot = equal(iota((fracs, SLOT), 0), frac)
        picked = dot(split_ref[...], onehot, NN)
        picked = picked[: 8 * GRID] + picked[8 * GRID : 16 * GRID] + picked[16 * GRID :]
        for c in range(2):
            row = jnp.zeros((GRID, SLOT), jnp.float32)
            for e in range(4):
                start = c * 4 * GRID + e * GRID
                row = jnp.where(edge == e, picked[start : start + GRID], row)
            rows_ref[d, c * GRID : (c + 1) * GRID, :] = row
            if c == 0:
                mean_ref[pl.ds(d, 1), :] = jnp.sum(row, 0, keepdims=True) * (1.0 / GRID)
        return carry

    lax.fori_loop(0, peers, one_peer, 0)


def means_body(peers, fracs, edges_ref, arrived_ref, mean_ref):
    means = [
        jnp.sum(edges_ref[e * GRID : (e + 1) * GRID, :], 0, keepdims=True) * (1.0 / GRID)
        for e in range(4)
    ]
    table = jnp.concatenate(means + means, 0)
    parts = jnp.concatenate(
        [p.astype(jnp.float32) for p in split3(table)] + [jnp.zeros_like(table)], 0
    ).astype(jnp.bfloat16)

    def one_peer(d, carry):
        edge, frac = edge_and_frac(arrived_ref[pl.ds(d, 1), :], fracs)
        picked = dot(parts, equal(iota((fracs, SLOT), 0), frac), NN)
        picked = picked[:8] + picked[8:16] + picked[16:24]
        mine = jnp.where(iota((8, SLOT), 0) == edge, picked, 0.0)
        mean_ref[pl.ds(d, 1), :] = jnp.sum(mine, 0, keepdims=True)
        return carry

    lax.fori_loop(0, peers, one_peer, 0)


def coarse_body(peers, high, mean_ref, other_ref, index_ref, weight_ref, corr_ref, out_ref):
    def tables(d):
        index = index_ref[pl.ds(d, 1), :]
        row = jnp.where(index >= 0, index >> 7, -1)
        lane = jnp.where(index >= 0, index & (LANES - 1), -1)
        return iota((high, SLOT), 0) == row, equal(iota((LANES, SLOT), 0), lane, jnp.float32)

    def collect(d, total):
        rows, lanes = tables(d)
        mismatch = mean_ref[pl.ds(d, 1), :] - other_ref[pl.ds(d, 1), :]
        return total + dot_exact(jnp.where(rows, mismatch, 0.0), lanes, NT)

    residual = lax.fori_loop(0, peers, collect, jnp.zeros((high, LANES), jnp.float32))
    correction = residual * weight_ref[...]
    corr_ref[...] = correction

    def pick(d, carry):
        rows, lanes = tables(d)
        picked = dot_exact(correction, lanes, NN)
        out_ref[pl.ds(d, 1), :] = jnp.sum(jnp.where(rows, picked, 0.0), 0, keepdims=True)
        return carry

    lax.fori_loop(0, peers, pick, 0)


def sweep_body(
    peers,
    fracs,
    rows_ref,
    extra_ref,
    arrived_ref,
    edges_ref,
    fields_ref,
    aperture_ref,
    source_ref,
    storage_ref,
    out_ref,
    sum_ref,
    count_ref,
    border_ref,
    side_ref,
):
    sum_ref[...] = jnp.zeros_like(sum_ref)
    count_ref[...] = jnp.zeros_like(count_ref)

    def one_peer(d, carry):
        edge, frac = edge_and_frac(arrived_ref[pl.ds(d, 1), :], fracs)
        onehot = equal(iota((fracs, SLOT), 0), frac)
        values = rows_ref[d] + extra_ref[pl.ds(d, 1), :]
        masked = []
        for c in range(2):
            for e in range(4):
                masked.append(jnp.where(edge == e, values[c * GRID : (c + 1) * GRID], 0.0))
        masked = jnp.concatenate(masked, 0)
        total = sum_ref[...]
        for part in split3(masked):
            total = total + dot(part, onehot, NT)
        sum_ref[...] = total
        count_ref[...] += dot(equal(iota((16, SLOT), 0), edge), onehot, NT)
        return carry

    lax.fori_loop(0, peers, one_peer, 0)
    for c in range(2):
        borders = []
        for e in range(4):
            start = (c * 4 + e) * GRID
            total = edges_ref[start : start + GRID, :] + sum_ref[start : start + GRID, :]
            borders.append(total / (1.0 + count_ref[e : e + 1, :]))
        border = jnp.transpose(jnp.concatenate(borders, 0))
        border_ref[c] = border
        parts = split3(border)
        for tile in range(TILES):
            row = iota((4 * GRID, LANES), 0)
            inject = edge_selector(tile) & (row >= 2 * GRID)
            inject = inject.astype(jnp.float32).astype(jnp.bfloat16)
            side = dot(parts[0], inject, NN) + dot(parts[1], inject, NN) + dot(parts[2], inject, NN)
            side_ref[c, :, tile * LANES : (tile + 1) * LANES] = side

    lane = iota((8, LANES), 1)
    column = lane & (GRID - 1)
    first, last = lane < GRID, lane >= LANES - GRID
    west_end, east_end = column == 0, column == GRID - 1

    def neighbours(x):
        down = [pltpu.roll(v, GRID, 1) for v in x]
        up = [pltpu.roll(v, LANES - GRID, 1) for v in x]
        above = [down[0]] + [jnp.where(first, down[t - 1], down[t]) for t in range(1, TILES)]
        below = [jnp.where(last, up[t + 1], up[t]) for t in range(TILES - 1)] + [up[-1]]
        left = [pltpu.roll(v, 1, 1) for v in x]
        right = [pltpu.roll(v, LANES - 1, 1) for v in x]
        return above, below, left, right

    def one_tile(i, carry):
        start = pl.multiple_of(i * 8, 8)
        here = pl.ds(start, 8)
        a = [aperture_ref[here, t * LANES : (t + 1) * LANES] for t in range(TILES)]
        above, below, left, right = neighbours(a)
        above[0] = jnp.where(first, a[0], above[0])
        below[-1] = jnp.where(last, a[-1], below[-1])
        w_up = [0.5 * (a[t] + above[t]) for t in range(TILES)]
        w_down = [0.5 * (a[t] + below[t]) for t in range(TILES)]
        w_left = [0.5 * (a[t] + jnp.where(west_end, a[t], left[t])) for t in range(TILES)]
        w_right = [0.5 * (a[t] + jnp.where(east_end, a[t], right[t])) for t in range(TILES)]
        for c in range(2):
            store = storage_ref[here, c : c + 1]
            border = border_ref[c, here, :]
            x, s, cu, cd, cl, cr = [], [], [], [], [], []
            for t in range(TILES):
                at = pl.ds(start * 2 * TILES + t * 2 + c, 8, stride=2 * TILES)
                inverse = 1.0 / (store + w_up[t] + w_down[t] + w_left[t] + w_right[t])
                side = side_ref[c, here, t * LANES : (t + 1) * LANES]
                value = source_ref[at, :] + side * jnp.where(west_end, w_left[t], w_right[t])
                up, down = w_up[t] * inverse, w_down[t] * inverse
                if t == 0:
                    value = value + jnp.where(first, border * w_up[t], 0.0)
                    up = jnp.where(first, 0.0, up)
                if t == TILES - 1:
                    bottom = pltpu.roll(border, 2 * GRID, 1)
                    value = value + jnp.where(last, bottom * w_down[t], 0.0)
                    down = jnp.where(last, 0.0, down)
                x.append(fields_ref[at, :])
                s.append(value * inverse)
                cu.append(up)
                cd.append(down)
                cl.append(jnp.where(west_end, 0.0, w_left[t] * inverse))
                cr.append(jnp.where(east_end, 0.0, w_right[t] * inverse))
            for sweep in range(SWEEPS):
                above, below, left, right = neighbours(x)
                x = [
                    (s[t] + cu[t] * above[t])
                    + (cd[t] * below[t] + (cl[t] * left[t] + cr[t] * right[t]))
                    for t in range(TILES)
                ]
            for t in range(TILES):
                at = pl.ds(start * 2 * TILES + t * 2 + c, 8, stride=2 * TILES)
                out_ref[at, :] = x[t]
        return carry

    lax.fori_loop(0, fracs // 8, one_tile, 0)


def call(body, shapes, scratch=()):
    return pl.pallas_call(
        body,
        out_shape=[jax.ShapeDtypeStruct(shape, dtype) for shape, dtype in shapes],
        scratch_shapes=list(scratch),
        compiler_params=pltpu.CompilerParams(vmem_limit_bytes=48 * 1024 * 1024),
    )


def exchange(x):
    return lax.all_to_all(x, AXES, split_axis=0, concat_axis=0, tiled=True)


def by_tiles(x):
    fracs = x.shape[0]
    return x.reshape(fracs, 2, TILES, LANES).transpose(0, 2, 1, 3).reshape(-1, LANES)


def shards(
    fields,
    aperture,
    source,
    storage,
    coarse_weight,
    source_slot,
    source_edge,
    destination,
    target_frac,
    target_edge,
    coarse_index,
):
    f32, i32 = jnp.float32, jnp.int32
    fracs = fields.shape[0]
    peers = lax.axis_size(AXES)
    coarse = coarse_weight.shape[0]
    per_dev = coarse // peers
    high = -(-per_dev // (8 * LANES)) * 8
    first = lax.axis_index(AXES) * per_dev
    local = coarse_index - first
    none = jnp.zeros_like(local)
    records = jnp.stack(
        [
            destination[:, 0],
            source_slot,
            source_edge,
            target_frac,
            target_edge + 1,
            local >> 7,
            local & (LANES - 1),
            none,
        ],
        0,
    )
    weight = lax.dynamic_slice(coarse_weight, (first,), (per_dev,))
    weight = jnp.pad(weight, (0, high * LANES - per_dev)).reshape(high, LANES)
    table = (peers, SLOT)
    sender, target, index = call(
        functools.partial(slots_body, peers, fracs), [(table, i32)] * 3
    )(records)
    arrived = exchange(target)
    state, sources = by_tiles(fields), by_tiles(source)
    for step in range(ITERS):
        edges, rows, mean = call(
            functools.partial(edges_body, peers, fracs),
            [((8 * GRID, fracs), f32), ((peers, 2 * GRID, SLOT), f32), (table, f32)],
            [pltpu.VMEM((24 * GRID, fracs), jnp.bfloat16)],
        )(state, sender)
        rows = exchange(rows)
        (own,) = call(functools.partial(means_body, peers, fracs), [(table, f32)])(edges, arrived)
        correction, extra = call(
            functools.partial(coarse_body, peers, high), [((high, LANES), f32), (table, f32)]
        )(mean, exchange(own), index, weight)
        (state,) = call(
            functools.partial(sweep_body, peers, fracs),
            [(state.shape, f32)],
            [
                pltpu.VMEM((8 * GRID, fracs), f32),
                pltpu.VMEM((16, fracs), f32),
                pltpu.VMEM((2, fracs, 4 * GRID), f32),
                pltpu.VMEM((2, fracs, GRID * GRID), f32),
            ],
        )(rows, exchange(extra), arrived, edges, state, aperture, sources, storage)
    blocks = lax.all_gather(correction, AXES, tiled=True)
    coarse_out = blocks.reshape(peers, high * LANES)[:, :per_dev].reshape(coarse)
    fields_out = state.reshape(fracs, TILES, 2, LANES).transpose(0, 2, 1, 3).reshape(fields.shape)
    return fields_out, coarse_out


def solution(mesh):
    every = P(AXES)
    return jax.shard_map(
        shards,
        mesh=mesh,
        in_specs=(
            P(AXES, None, None),
            P(AXES, None),
            P(AXES, None, None),
            P(AXES, None),
            P(),
            every,
            every,
            P(AXES, None),
            every,
            every,
            every,
        ),
        out_specs=(P(AXES, None, None), P()),
        check_vma=False,
    )
```

```python
import functools

import jax
import jax.numpy as jnp
from jax import lax
from jax.experimental import pallas as pl
from jax.experimental.pallas import tpu as pltpu
from jax.sharding import PartitionSpec as P

GRID = 32
ITERS = 2
SWEEPS = 8
SLOT = 128
LANES = 128
TILES = GRID * GRID // LANES
GROUP = 8
AXES = ("gx", "gy")
NT = (((1,), (1,)), ((), ()))
NN = (((1,), (0,)), ((), ()))


def dot(a, b, dims):
    return lax.dot_general(a, b, dims, preferred_element_type=jnp.float32)


def split3(x):
    high = x.astype(jnp.bfloat16)
    rest = x - high.astype(jnp.float32)
    mid = rest.astype(jnp.bfloat16)
    low = (rest - mid.astype(jnp.float32)).astype(jnp.bfloat16)
    return high, mid, low


def iota(shape, dim):
    return lax.broadcasted_iota(jnp.int32, shape, dim)


def equal(a, b, dtype=jnp.bfloat16):
    return jnp.where(a == b, 1.0, 0.0).astype(dtype)


def slots_body(peers, fracs, record_ref, sender_ref, target_ref, coarse_ref):
    chunk = 512
    count = record_ref.shape[1]
    upto = (iota((chunk, chunk), 0) <= iota((chunk, chunk), 1)).astype(jnp.float32)
    upto = upto.astype(jnp.bfloat16)
    base = jnp.zeros((peers, 1), jnp.float32)
    total = jnp.zeros((6 * peers, SLOT), jnp.float32)
    for start in range(0, count, chunk):
        rows = [record_ref[i : i + 1, start : start + chunk] for i in range(7)]
        onehot = equal(iota((peers, chunk), 0), rows[0], jnp.float32)
        running = dot(onehot.astype(jnp.bfloat16), upto, NN)
        place = jnp.sum(onehot * (running + base), 0, keepdims=True) - 1.0
        base = base + running[:, chunk - 1 :]
        at_place = equal(iota((SLOT, chunk), 0), place.astype(jnp.int32))
        parts = [onehot * rows[i].astype(jnp.float32) for i in range(1, 7)]
        total = total + dot(jnp.concatenate(parts, 0).astype(jnp.bfloat16), at_place, NT)
    table = (total + 0.5).astype(jnp.int32)
    pieces = [table[i * peers : (i + 1) * peers] for i in range(6)]
    valid = pieces[3] > 0
    sender_ref[...] = jnp.where(valid, pieces[1] * fracs + pieces[0], -1)
    target_ref[...] = jnp.where(valid, (pieces[3] - 1) * fracs + pieces[2], -1)
    coarse_ref[...] = jnp.where(valid, pieces[4] * LANES + pieces[5], -1)


def edge_selector(tile):
    row = iota((4 * GRID, LANES), 0)
    k, edge = row & (GRID - 1), row >> 5
    cell = jnp.where(
        edge == 0,
        k,
        jnp.where(edge == 1, GRID * (GRID - 1) + k, k * GRID + (edge - 2) * (GRID - 1)),
    )
    return (iota((4 * GRID, LANES), 1) + tile * LANES) == cell


def edge_and_frac(code, fracs):
    shift = fracs.bit_length() - 1
    return jnp.where(code >= 0, code >> shift, -1), jnp.where(code >= 0, code & (fracs - 1), -1)


def edges_body(peers, fracs, fields_ref, sender_ref, edges_ref, rows_ref, mean_ref, split_ref):
    for c in range(2):
        total = jnp.zeros((4 * GRID, fracs), jnp.float32)
        for tile in range(TILES):
            cells = fields_ref[pl.ds(tile * 2 + c, fracs, stride=2 * TILES), :]
            selector = edge_selector(tile).astype(jnp.float32).astype(jnp.bfloat16)
            for part in split3(cells):
                total = total + dot(selector, part, NT)
        edges_ref[c * 4 * GRID : (c + 1) * 4 * GRID, :] = total
        for i, part in enumerate(split3(total)):
            start = i * 8 * GRID + c * 4 * GRID
            split_ref[start : start + 4 * GRID, :] = part

    def one_pair(d):
        codes = jnp.concatenate([sender_ref[pl.ds(d + i, 1), :] for i in range(2)], 1)
        edge, frac = edge_and_frac(codes, fracs)
        onehot = equal(iota((fracs, 2 * SLOT), 0), frac)
        picked = dot(split_ref[...], onehot, NN)
        picked = picked[: 8 * GRID] + picked[8 * GRID : 16 * GRID] + picked[16 * GRID :]
        for c in range(2):
            row = jnp.zeros((GRID, 2 * SLOT), jnp.float32)
            for e in range(4):
                start = c * 4 * GRID + e * GRID
                row = jnp.where(edge == e, picked[start : start + GRID], row)
            for i in range(2):
                half = row[:, i * SLOT : (i + 1) * SLOT]
                rows_ref[d + i, c * GRID : (c + 1) * GRID, :] = half
                if c == 0:
                    mean = jnp.sum(half, 0, keepdims=True) * (1.0 / GRID)
                    mean_ref[pl.ds(d + i, 1), :] = mean

    def pairs(g, carry):
        one_pair(g * 4)
        one_pair(g * 4 + 2)
        return carry

    lax.fori_loop(0, peers // 4, pairs, 0)


def lanes_of(ref, start, rows=None):
    if rows is None:
        return jnp.concatenate([ref[pl.ds(start + i, 1), :] for i in range(GROUP)], 1)
    return jnp.concatenate([ref[start + i, rows] for i in range(GROUP)], 1)


def stacked3(x):
    parts = [p.astype(jnp.float32) for p in split3(x)] + [jnp.zeros_like(x)]
    return jnp.concatenate(parts, 0).astype(jnp.bfloat16)


def sum3(x):
    return x[:8] + x[8:16] + x[16:24]


def traffic_body(
    peers,
    columns,
    fracs,
    high,
    rows_ref,
    mean_ref,
    edges_ref,
    arrived_ref,
    index_ref,
    weight_ref,
    rows_out,
    extra_out,
    own_send,
    own_recv,
    extra_send,
    send_sem,
    recv_sem,
):
    me = lax.axis_index(AXES[0]) * columns + lax.axis_index(AXES[1])

    def device(step):
        target = lax.rem(me + step, peers)
        return target, (target // columns, lax.rem(target, columns))

    barrier = pltpu.get_barrier_semaphore()

    def greet(step, carry):
        pl.semaphore_signal(
            barrier, inc=1, device_id=device(step)[1], device_id_type=pl.DeviceIdType.MESH
        )
        return carry

    lax.fori_loop(1, peers, greet, 0)
    pl.semaphore_wait(barrier, peers - 1)

    def send_all(source, target, kind):
        def one(step, carry):
            there, device_id = device(step)
            pltpu.make_async_remote_copy(
                src_ref=source.at[there],
                dst_ref=target.at[me],
                send_sem=send_sem.at[kind],
                recv_sem=recv_sem.at[kind],
                device_id=device_id,
                device_id_type=pl.DeviceIdType.MESH,
            ).start()
            return carry

        lax.fori_loop(1, peers, one, 0)
        target[me] = source[me]

    def wait_all(ref, sem):
        others = ref.at[pl.ds(0, peers - 1)]
        pltpu.make_async_copy(others, others, sem).wait()

    send_all(rows_ref, rows_out, 0)

    means = [
        jnp.sum(edges_ref[e * GRID : (e + 1) * GRID, :], 0, keepdims=True) * (1.0 / GRID)
        for e in range(4)
    ]
    parts = stacked3(jnp.concatenate(means + means, 0))
    wide = GROUP * SLOT

    def own_means(g, carry):
        edge, frac = edge_and_frac(lanes_of(arrived_ref, g * GROUP), fracs)
        picked = sum3(dot(parts, equal(iota((fracs, wide), 0), frac), NN))
        mine = jnp.sum(jnp.where(iota((8, wide), 0) == edge, picked, 0.0), 0, keepdims=True)
        for i in range(GROUP):
            own_send[g * GROUP + i] = mine[:, i * SLOT : (i + 1) * SLOT]
        return carry

    lax.fori_loop(0, peers // GROUP, own_means, 0)
    send_all(own_send, own_recv, 1)
    wait_all(own_recv, recv_sem.at[1])

    def tables(g):
        index = lanes_of(index_ref, g * GROUP)
        row = jnp.where(index >= 0, index >> 7, -1)
        lane = jnp.where(index >= 0, index & (LANES - 1), -1)
        return iota((8, wide), 0) == row, equal(iota((LANES, wide), 0), lane)

    def collect(g, total):
        rows, onehot = tables(g)
        other = jnp.concatenate([own_recv[g * GROUP + i] for i in range(GROUP)], 1)
        mismatch = lanes_of(mean_ref, g * GROUP) - other
        return total + dot(stacked3(jnp.where(rows, mismatch, 0.0)), onehot, NT)

    residual = lax.fori_loop(0, peers // GROUP, collect, jnp.zeros((32, LANES), jnp.float32))
    correction = sum3(residual) * weight_ref[...]
    halves = stacked3(correction)

    def pick(g, carry):
        rows, onehot = tables(g)
        picked = jnp.where(rows, sum3(dot(halves, onehot, NN)), 0.0)
        mine = jnp.sum(picked, 0, keepdims=True)
        for i in range(GROUP):
            extra_send[g * GROUP + i] = jnp.where(
                iota((8, SLOT), 0) == high, mine[:, i * SLOT : (i + 1) * SLOT], correction
            )
        return carry

    lax.fori_loop(0, peers // GROUP, pick, 0)
    send_all(extra_send, extra_out, 2)
    wait_all(extra_out, recv_sem.at[2])
    wait_all(rows_out, recv_sem.at[0])
    for kind, ref in ((0, rows_out), (1, own_recv), (2, extra_out)):
        wait_all(ref, send_sem.at[kind])


def sweep_body(
    peers,
    fracs,
    high,
    rows_ref,
    extra_ref,
    arrived_ref,
    edges_ref,
    fields_ref,
    aperture_ref,
    source_ref,
    storage_ref,
    out_ref,
    sum_ref,
    count_ref,
    border_ref,
    side_ref,
):
    sum_ref[...] = jnp.zeros_like(sum_ref)
    count_ref[...] = jnp.zeros_like(count_ref)

    wide = GROUP * SLOT

    def one_group(g, carry):
        edge, frac = edge_and_frac(lanes_of(arrived_ref, g * GROUP), fracs)
        onehot = equal(iota((fracs, wide), 0), frac)
        extra = lanes_of(extra_ref, g * GROUP, slice(high, high + 1))
        values = lanes_of(rows_ref, g * GROUP, slice(0, 2 * GRID)) + extra
        masked = []
        for c in range(2):
            for e in range(4):
                masked.append(jnp.where(edge == e, values[c * GRID : (c + 1) * GRID], 0.0))
        parts = split3(jnp.concatenate(masked, 0))
        sum_ref[...] += dot(jnp.concatenate(parts, 0), onehot, NT)
        count_ref[...] += dot(equal(iota((16, wide), 0), edge), onehot, NT)
        return carry

    lax.fori_loop(0, peers // GROUP, one_group, 0)
    for c in range(2):
        borders = []
        for e in range(4):
            start = (c * 4 + e) * GRID
            total = edges_ref[start : start + GRID, :]
            for i in range(3):
                part = start + i * 8 * GRID
                total = total + sum_ref[part : part + GRID, :]
            borders.append(total / (1.0 + count_ref[e : e + 1, :]))
        border = jnp.transpose(jnp.concatenate(borders, 0))
        border_ref[c] = border
        parts = split3(border)
        for tile in range(TILES):
            row = iota((4 * GRID, LANES), 0)
            inject = edge_selector(tile) & (row >= 2 * GRID)
            inject = inject.astype(jnp.float32).astype(jnp.bfloat16)
            side = dot(parts[0], inject, NN) + dot(parts[1], inject, NN) + dot(parts[2], inject, NN)
            side_ref[c, :, tile * LANES : (tile + 1) * LANES] = side

    lane = iota((8, LANES), 1)
    column = lane & (GRID - 1)
    first, last = lane < GRID, lane >= LANES - GRID
    west_end, east_end = column == 0, column == GRID - 1

    def neighbours(x):
        down = [pltpu.roll(v, GRID, 1) for v in x]
        up = [pltpu.roll(v, LANES - GRID, 1) for v in x]
        above = [down[0]] + [jnp.where(first, down[t - 1], down[t]) for t in range(1, TILES)]
        below = [jnp.where(last, up[t + 1], up[t]) for t in range(TILES - 1)] + [up[-1]]
        left = [pltpu.roll(v, 1, 1) for v in x]
        right = [pltpu.roll(v, LANES - 1, 1) for v in x]
        return above, below, left, right

    def one_tile(i, carry):
        start = pl.multiple_of(i * 8, 8)
        here = pl.ds(start, 8)
        a = [aperture_ref[here, t * LANES : (t + 1) * LANES] for t in range(TILES)]
        above, below, left, right = neighbours(a)
        above[0] = jnp.where(first, a[0], above[0])
        below[-1] = jnp.where(last, a[-1], below[-1])
        w_up = [0.5 * (a[t] + above[t]) for t in range(TILES)]
        w_down = [0.5 * (a[t] + below[t]) for t in range(TILES)]
        w_left = [0.5 * (a[t] + jnp.where(west_end, a[t], left[t])) for t in range(TILES)]
        w_right = [0.5 * (a[t] + jnp.where(east_end, a[t], right[t])) for t in range(TILES)]
        fields = []
        for c in range(2):
            store = storage_ref[here, c : c + 1]
            border = border_ref[c, here, :]
            x, s, cu, cd, cl, cr = [], [], [], [], [], []
            for t in range(TILES):
                at = pl.ds(start * 2 * TILES + t * 2 + c, 8, stride=2 * TILES)
                inverse = 1.0 / (store + w_up[t] + w_down[t] + w_left[t] + w_right[t])
                side = side_ref[c, here, t * LANES : (t + 1) * LANES]
                value = source_ref[at, :] + side * jnp.where(west_end, w_left[t], w_right[t])
                up, down = w_up[t] * inverse, w_down[t] * inverse
                if t == 0:
                    value = value + jnp.where(first, border * w_up[t], 0.0)
                    up = jnp.where(first, 0.0, up)
                if t == TILES - 1:
                    bottom = pltpu.roll(border, 2 * GRID, 1)
                    value = value + jnp.where(last, bottom * w_down[t], 0.0)
                    down = jnp.where(last, 0.0, down)
                x.append(fields_ref[at, :])
                s.append(value * inverse)
                cu.append(up)
                cd.append(down)
                cl.append(jnp.where(west_end, 0.0, w_left[t] * inverse))
                cr.append(jnp.where(east_end, 0.0, w_right[t] * inverse))
            fields.append((x, s, cu, cd, cl, cr))
        state = [f[0] for f in fields]
        for sweep in range(SWEEPS):
            for c in range(2):
                above, below, left, right = neighbours(state[c])
                _, s, cu, cd, cl, cr = fields[c]
                state[c] = [
                    (s[t] + cu[t] * above[t])
                    + (cd[t] * below[t] + (cl[t] * left[t] + cr[t] * right[t]))
                    for t in range(TILES)
                ]
        for c in range(2):
            for t in range(TILES):
                at = pl.ds(start * 2 * TILES + t * 2 + c, 8, stride=2 * TILES)
                out_ref[at, :] = state[c][t]
        return carry

    lax.fori_loop(0, fracs // 8, one_tile, 0)


def call(body, shapes, scratch=(), **params):
    return pl.pallas_call(
        body,
        out_shape=[jax.ShapeDtypeStruct(shape, dtype) for shape, dtype in shapes],
        scratch_shapes=list(scratch),
        compiler_params=pltpu.CompilerParams(vmem_limit_bytes=48 * 1024 * 1024, **params),
    )


def exchange(x):
    return lax.all_to_all(x, AXES, split_axis=0, concat_axis=0, tiled=True)


def by_tiles(x):
    fracs = x.shape[0]
    return x.reshape(fracs, 2, TILES, LANES).transpose(0, 2, 1, 3).reshape(-1, LANES)


def shards(
    fields,
    aperture,
    source,
    storage,
    coarse_weight,
    source_slot,
    source_edge,
    destination,
    target_frac,
    target_edge,
    coarse_index,
):
    f32, i32 = jnp.float32, jnp.int32
    fracs = fields.shape[0]
    peers = lax.axis_size(AXES)
    coarse = coarse_weight.shape[0]
    per_dev = coarse // peers
    high = -(-per_dev // LANES)
    columns = lax.axis_size(AXES[1])
    first = lax.axis_index(AXES) * per_dev
    local = coarse_index - first
    none = jnp.zeros_like(local)
    records = jnp.stack(
        [
            destination[:, 0],
            source_slot,
            source_edge,
            target_frac,
            target_edge + 1,
            local >> 7,
            local & (LANES - 1),
            none,
        ],
        0,
    )
    weight = lax.dynamic_slice(coarse_weight, (first,), (per_dev,))
    weight = jnp.pad(weight, (0, 8 * LANES - per_dev)).reshape(8, LANES)
    table = (peers, SLOT)
    sender, target, index = call(
        functools.partial(slots_body, peers, fracs), [(table, i32)] * 3
    )(records)
    arrived = exchange(target)
    state, sources = by_tiles(fields), by_tiles(source)
    for step in range(ITERS):
        edges, rows, mean = call(
            functools.partial(edges_body, peers, fracs),
            [((8 * GRID, fracs), f32), ((peers, 2 * GRID, SLOT), f32), (table, f32)],
            [pltpu.VMEM((24 * GRID, fracs), jnp.bfloat16)],
        )(state, sender)
        rows, extra = call(
            functools.partial(traffic_body, peers, columns, fracs, high),
            [((peers, 2 * GRID, SLOT), f32), ((peers, 8, LANES), f32)],
            [
                pltpu.VMEM((peers, 1, SLOT), f32),
                pltpu.VMEM((peers, 1, SLOT), f32),
                pltpu.VMEM((peers, 8, LANES), f32),
                pltpu.SemaphoreType.DMA((3,)),
                pltpu.SemaphoreType.DMA((3,)),
            ],
            collective_id=0,
            has_side_effects=True,
        )(rows, mean, edges, arrived, index, weight)
        (state,) = call(
            functools.partial(sweep_body, peers, fracs, high),
            [(state.shape, f32)],
            [
                pltpu.VMEM((24 * GRID, fracs), f32),
                pltpu.VMEM((16, fracs), f32),
                pltpu.VMEM((2, fracs, 4 * GRID), f32),
                pltpu.VMEM((2, fracs, GRID * GRID), f32),
            ],
        )(rows, extra, arrived, edges, state, aperture, sources, storage)
    coarse_out = extra.reshape(peers, 8 * LANES)[:, :per_dev].reshape(coarse)
    fields_out = state.reshape(fracs, TILES, 2, LANES).transpose(0, 2, 1, 3).reshape(fields.shape)
    return fields_out, coarse_out


def solution(mesh):
    every = P(AXES)
    return jax.shard_map(
        shards,
        mesh=mesh,
        in_specs=(
            P(AXES, None, None),
            P(AXES, None),
            P(AXES, None, None),
            P(AXES, None),
            P(),
            every,
            every,
            P(AXES, None),
            every,
            every,
            every,
        ),
        out_specs=(P(AXES, None, None), P()),
        check_vma=False,
    )
```

```python
import functools

import jax
import jax.numpy as jnp
from jax import lax
from jax.experimental import pallas as pl
from jax.experimental.pallas import tpu as pltpu
from jax.sharding import PartitionSpec as P

GRID = 32
ITERS = 2
SWEEPS = 8
SLOT = 128
LANES = 128
TILES = GRID * GRID // LANES
GROUP = 8
AXES = ("gx", "gy")
NT = (((1,), (1,)), ((), ()))
NN = (((1,), (0,)), ((), ()))


def dot(a, b, dims):
    return lax.dot_general(a, b, dims, preferred_element_type=jnp.float32)


def split3(x):
    high = x.astype(jnp.bfloat16)
    rest = x - high.astype(jnp.float32)
    mid = rest.astype(jnp.bfloat16)
    low = (rest - mid.astype(jnp.float32)).astype(jnp.bfloat16)
    return high, mid, low


def iota(shape, dim):
    return lax.broadcasted_iota(jnp.int32, shape, dim)


def equal(a, b, dtype=jnp.bfloat16):
    return jnp.where(a == b, 1.0, 0.0).astype(dtype)


def slots_body(peers, fracs, record_ref, sender_ref, target_ref, coarse_ref):
    chunk = 512
    count = record_ref.shape[1]
    upto = (iota((chunk, chunk), 0) <= iota((chunk, chunk), 1)).astype(jnp.float32)
    upto = upto.astype(jnp.bfloat16)
    base = jnp.zeros((peers, 1), jnp.float32)
    total = jnp.zeros((6 * peers, SLOT), jnp.float32)
    for start in range(0, count, chunk):
        rows = [record_ref[i : i + 1, start : start + chunk] for i in range(7)]
        onehot = equal(iota((peers, chunk), 0), rows[0], jnp.float32)
        running = dot(onehot.astype(jnp.bfloat16), upto, NN)
        place = jnp.sum(onehot * (running + base), 0, keepdims=True) - 1.0
        base = base + running[:, chunk - 1 :]
        at_place = equal(iota((SLOT, chunk), 0), place.astype(jnp.int32))
        parts = [onehot * rows[i].astype(jnp.float32) for i in range(1, 7)]
        total = total + dot(jnp.concatenate(parts, 0).astype(jnp.bfloat16), at_place, NT)
    table = (total + 0.5).astype(jnp.int32)
    pieces = [table[i * peers : (i + 1) * peers] for i in range(6)]
    valid = pieces[3] > 0
    sender_ref[...] = jnp.where(valid, pieces[1] * fracs + pieces[0], -1)
    target_ref[...] = jnp.where(valid, (pieces[3] - 1) * fracs + pieces[2], -1)
    coarse_ref[...] = jnp.where(valid, pieces[4] * LANES + pieces[5], -1)


def edge_and_frac(code, fracs):
    shift = fracs.bit_length() - 1
    return jnp.where(code >= 0, code >> shift, -1), jnp.where(code >= 0, code & (fracs - 1), -1)


def take_edges(cells_ref, edges_ref):
    size = GRID * GRID
    for c in range(2):
        views = (
            pl.ds(c * size, GRID),
            pl.ds(c * size + size - GRID, GRID),
            pl.ds(c * size, GRID, stride=GRID),
            pl.ds(c * size + GRID - 1, GRID, stride=GRID),
        )
        for g in range(cells_ref.shape[0]):
            lanes = slice(g * LANES, (g + 1) * LANES)
            for e in range(4):
                start = (c * 4 + e) * GRID
                edges_ref[start : start + GRID, lanes] = cells_ref[g, views[e], :]


def tile_rows(g, tile, c):
    return pl.ds(g * LANES * 2 * TILES + tile * 2 + c, LANES, stride=2 * TILES)


def turn_body(fields_ref, source_ref, aperture_ref, cells_ref, sources_ref, openings_ref, edges_ref):
    for g in range(aperture_ref.shape[0] // LANES):
        lanes = slice(g * LANES, (g + 1) * LANES)
        for tile in range(TILES):
            there = slice(tile * LANES, (tile + 1) * LANES)
            openings_ref[g, there, :] = jnp.transpose(aperture_ref[lanes, there])
            for c in range(2):
                row = c * GRID * GRID + tile * LANES
                cells = jnp.transpose(fields_ref[tile_rows(g, tile, c), :])
                cells_ref[g, row : row + LANES, :] = cells
                cells = jnp.transpose(source_ref[tile_rows(g, tile, c), :])
                sources_ref[g, row : row + LANES, :] = cells
    take_edges(cells_ref, edges_ref)


def gather_body(peers, fracs, edges_ref, sender_ref, rows_ref, mean_ref, split_ref):
    for i, part in enumerate(split3(edges_ref[...])):
        split_ref[i * 8 * GRID : (i + 1) * 8 * GRID, :] = part

    def one_pair(d):
        codes = jnp.concatenate([sender_ref[pl.ds(d + i, 1), :] for i in range(2)], 1)
        edge, frac = edge_and_frac(codes, fracs)
        onehot = equal(iota((fracs, 2 * SLOT), 0), frac)
        picked = dot(split_ref[...], onehot, NN)
        picked = picked[: 8 * GRID] + picked[8 * GRID : 16 * GRID] + picked[16 * GRID :]
        for c in range(2):
            row = jnp.zeros((GRID, 2 * SLOT), jnp.float32)
            for e in range(4):
                start = c * 4 * GRID + e * GRID
                row = jnp.where(edge == e, picked[start : start + GRID], row)
            for i in range(2):
                half = row[:, i * SLOT : (i + 1) * SLOT]
                rows_ref[d + i, c * GRID : (c + 1) * GRID, :] = half
                if c == 0:
                    mean = jnp.sum(half, 0, keepdims=True) * (1.0 / GRID)
                    mean_ref[pl.ds(d + i, 1), :] = mean

    def pairs(g, carry):
        one_pair(g * 4)
        one_pair(g * 4 + 2)
        return carry

    lax.fori_loop(0, peers // 4, pairs, 0)


def lanes_of(ref, start, rows=None):
    if rows is None:
        return jnp.concatenate([ref[pl.ds(start + i, 1), :] for i in range(GROUP)], 1)
    return jnp.concatenate([ref[start + i, rows] for i in range(GROUP)], 1)


def stacked3(x):
    parts = [p.astype(jnp.float32) for p in split3(x)] + [jnp.zeros_like(x)]
    return jnp.concatenate(parts, 0).astype(jnp.bfloat16)


def sum3(x):
    return x[:8] + x[8:16] + x[16:24]


def traffic_body(
    peers,
    columns,
    fracs,
    high,
    rows_ref,
    mean_ref,
    edges_ref,
    arrived_ref,
    index_ref,
    weight_ref,
    rows_out,
    extra_out,
    own_send,
    own_recv,
    extra_send,
    send_sem,
    recv_sem,
):
    me = lax.axis_index(AXES[0]) * columns + lax.axis_index(AXES[1])

    def device(step):
        target = lax.rem(me + step, peers)
        return target, (target // columns, lax.rem(target, columns))

    barrier = pltpu.get_barrier_semaphore()

    def greet(step, carry):
        pl.semaphore_signal(
            barrier, inc=1, device_id=device(step)[1], device_id_type=pl.DeviceIdType.MESH
        )
        return carry

    lax.fori_loop(1, peers, greet, 0)
    pl.semaphore_wait(barrier, peers - 1)

    def send_some(source, target, kind, begin, end):
        def one(step, carry):
            there, device_id = device(step)
            pltpu.make_async_remote_copy(
                src_ref=source.at[there],
                dst_ref=target.at[me],
                send_sem=send_sem.at[kind],
                recv_sem=recv_sem.at[kind],
                device_id=device_id,
                device_id_type=pl.DeviceIdType.MESH,
            ).start()
            return carry

        lax.fori_loop(begin, end, one, 0)

    def send_all(source, target, kind):
        send_some(source, target, kind, 1, peers)
        target[me] = source[me]

    def wait_all(ref, sem):
        others = ref.at[pl.ds(0, peers - 1)]
        pltpu.make_async_copy(others, others, sem).wait()

    means = [
        jnp.sum(edges_ref[e * GRID : (e + 1) * GRID, :], 0, keepdims=True) * (1.0 / GRID)
        for e in range(4)
    ]
    parts = stacked3(jnp.concatenate(means + means, 0))
    wide = GROUP * SLOT

    def own_means(g, carry):
        edge, frac = edge_and_frac(lanes_of(arrived_ref, g * GROUP), fracs)
        picked = sum3(dot(parts, equal(iota((fracs, wide), 0), frac), NN))
        mine = jnp.sum(jnp.where(iota((8, wide), 0) == edge, picked, 0.0), 0, keepdims=True)
        for i in range(GROUP):
            own_send[g * GROUP + i] = mine[:, i * SLOT : (i + 1) * SLOT]
        return carry

    lax.fori_loop(0, peers // GROUP, own_means, 0)
    send_all(own_send, own_recv, 1)
    early = peers // 3
    send_some(rows_ref, rows_out, 0, 1, early)
    wait_all(own_recv, recv_sem.at[1])

    def tables(g):
        index = lanes_of(index_ref, g * GROUP)
        row = jnp.where(index >= 0, index >> 7, -1)
        lane = jnp.where(index >= 0, index & (LANES - 1), -1)
        return iota((8, wide), 0) == row, equal(iota((LANES, wide), 0), lane)

    def collect(g, total):
        rows, onehot = tables(g)
        other = jnp.concatenate([own_recv[g * GROUP + i] for i in range(GROUP)], 1)
        mismatch = lanes_of(mean_ref, g * GROUP) - other
        return total + dot(stacked3(jnp.where(rows, mismatch, 0.0)), onehot, NT)

    residual = lax.fori_loop(0, peers // GROUP, collect, jnp.zeros((32, LANES), jnp.float32))
    correction = sum3(residual) * weight_ref[...]
    halves = stacked3(correction)

    def pick(g, carry):
        rows, onehot = tables(g)
        picked = jnp.where(rows, sum3(dot(halves, onehot, NN)), 0.0)
        mine = jnp.sum(picked, 0, keepdims=True)
        for i in range(GROUP):
            extra_send[g * GROUP + i] = jnp.where(
                iota((8, SLOT), 0) == high, mine[:, i * SLOT : (i + 1) * SLOT], correction
            )
        return carry

    lax.fori_loop(0, peers // GROUP, pick, 0)
    send_all(extra_send, extra_out, 2)
    send_some(rows_ref, rows_out, 0, early, peers)
    rows_out[me] = rows_ref[me]
    wait_all(extra_out, recv_sem.at[2])
    wait_all(rows_out, recv_sem.at[0])
    for kind, ref in ((0, rows_out), (1, own_recv), (2, extra_out)):
        wait_all(ref, send_sem.at[kind])


def sweep_body(
    peers,
    fracs,
    high,
    last,
    rows_ref,
    extra_ref,
    arrived_ref,
    edges_ref,
    cells_ref,
    openings_ref,
    sources_ref,
    storage_ref,
    *refs,
):
    if last:
        (out_ref,), scratch = refs[:1], refs[1:]
        new_ref, scratch = scratch[-1], scratch[:-1]
    else:
        (new_ref, new_edges_ref), scratch = refs[:2], refs[2:]
    sum_ref, count_ref, border_ref, open_ref, even_ref, odd_ref, s_ref = scratch[:7]
    up_ref, down_ref, left_ref, right_ref = scratch[7:]
    sum_ref[...] = jnp.zeros_like(sum_ref)
    count_ref[...] = jnp.zeros_like(count_ref)

    wide = GROUP * SLOT

    def one_group(g, carry):
        edge, frac = edge_and_frac(lanes_of(arrived_ref, g * GROUP), fracs)
        onehot = equal(iota((fracs, wide), 0), frac)
        extra = lanes_of(extra_ref, g * GROUP, slice(high, high + 1))
        values = lanes_of(rows_ref, g * GROUP, slice(0, 2 * GRID)) + extra
        masked = []
        for c in range(2):
            for e in range(4):
                masked.append(jnp.where(edge == e, values[c * GRID : (c + 1) * GRID], 0.0))
        parts = split3(jnp.concatenate(masked, 0))
        sum_ref[...] += dot(jnp.concatenate(parts, 0), onehot, NT)
        count_ref[...] += dot(equal(iota((16, wide), 0), edge), onehot, NT)
        return carry

    lax.fori_loop(0, peers // GROUP, one_group, 0)
    for c in range(2):
        for e in range(4):
            start = (c * 4 + e) * GRID
            total = edges_ref[start : start + GRID, :]
            for i in range(3):
                part = start + i * 8 * GRID
                total = total + sum_ref[part : part + GRID, :]
            total = total / (1.0 + count_ref[e : e + 1, :])
            for g in range(fracs // LANES):
                border_ref[g, start : start + GRID, :] = total[:, g * LANES : (g + 1) * LANES]

    size = GRID * GRID
    sublane = iota((8, LANES), 0)
    top, bottom = sublane == 0, sublane == TILES - 1
    groups = fracs // LANES

    def fill_ends(ref, start, count):
        for j in range(start, start + count):
            if j < GRID:
                ref[GRID + LANES + j] = pltpu.roll(ref[GRID + j], TILES - 1, 0)
            if j >= LANES - GRID:
                ref[j - (LANES - GRID)] = pltpu.roll(ref[GRID + j], 1, 0)

    def one_block(i, carry):
        c, g = i // groups, lax.rem(i, groups)
        for j in range(LANES):
            at = pl.ds(j, TILES, stride=LANES)
            open_ref[GRID + j] = openings_ref[g, at, :]
            even_ref[GRID + j] = cells_ref[g, pl.ds(c * size + j, TILES, stride=LANES), :]
        fill_ends(open_ref, 0, LANES)
        fill_ends(even_ref, 0, LANES)
        store = storage_ref[i]
        base = c * 4 * GRID
        for j in range(LANES):
            row, column = j // GRID, j % GRID
            here = open_ref[GRID + j]
            above, below = open_ref[j], open_ref[2 * GRID + j]
            if row == 0:
                above = jnp.where(top, here, above)
            if row == LANES // GRID - 1:
                below = jnp.where(bottom, here, below)
            w_up, w_down = 0.5 * (here + above), 0.5 * (here + below)
            w_left = here if column == 0 else 0.5 * (here + open_ref[GRID + j - 1])
            w_right = here if column == GRID - 1 else 0.5 * (here + open_ref[GRID + j + 1])
            inverse = 1.0 / (store + w_up + w_down + w_left + w_right)
            value = sources_ref[g, pl.ds(c * size + j, TILES, stride=LANES), :] * inverse
            w_up, w_down = w_up * inverse, w_down * inverse
            w_left, w_right = w_left * inverse, w_right * inverse
            if row == 0:
                side = border_ref[g, pl.ds(base + column, 1), :]
                value = value + jnp.where(top, w_up * side, 0.0)
                w_up = jnp.where(top, 0.0, w_up)
            if row == LANES // GRID - 1:
                side = border_ref[g, pl.ds(base + GRID + column, 1), :]
                value = value + jnp.where(bottom, w_down * side, 0.0)
                w_down = jnp.where(bottom, 0.0, w_down)
            step = LANES // GRID
            if column == 0:
                side = border_ref[g, pl.ds(base + 2 * GRID + row, TILES, stride=step), :]
                value = value + w_left * side
                w_left = jnp.zeros_like(w_left)
            if column == GRID - 1:
                side = border_ref[g, pl.ds(base + 3 * GRID + row, TILES, stride=step), :]
                value = value + w_right * side
                w_right = jnp.zeros_like(w_right)
            s_ref[j] = value
            up_ref[j], down_ref[j] = w_up, w_down
            left_ref[j], right_ref[j] = w_left, w_right

        def one_sweep(old, new):
            for j in range(LANES):
                new[GRID + j] = (s_ref[j] + up_ref[j] * old[j]) + (
                    down_ref[j] * old[2 * GRID + j]
                    + (left_ref[j] * old[GRID + j - 1] + right_ref[j] * old[GRID + j + 1])
                )
                fill_ends(new, j, 1)

        def two_sweeps(k, carry):
            one_sweep(even_ref, odd_ref)
            one_sweep(odd_ref, even_ref)
            return carry

        lax.fori_loop(0, SWEEPS // 2, two_sweeps, 0)
        for j in range(LANES):
            new_ref[g, pl.ds(c * size + j, TILES, stride=LANES), :] = even_ref[GRID + j]
        return carry

    lax.fori_loop(0, 2 * groups, one_block, 0)
    if not last:
        take_edges(new_ref, new_edges_ref)
        return
    for c in range(2):
        for g in range(groups):
            for tile in range(TILES):
                row = c * size + tile * LANES
                cells = new_ref[g, row : row + LANES, :]
                out_ref[tile_rows(g, tile, c), :] = jnp.transpose(cells)


def call(body, shapes, scratch=(), **params):
    return pl.pallas_call(
        body,
        out_shape=[jax.ShapeDtypeStruct(shape, dtype) for shape, dtype in shapes],
        scratch_shapes=list(scratch),
        compiler_params=pltpu.CompilerParams(vmem_limit_bytes=40 * 1024 * 1024, **params),
    )


def exchange(x):
    return lax.all_to_all(x, AXES, split_axis=0, concat_axis=0, tiled=True)


def by_tiles(x):
    fracs = x.shape[0]
    return x.reshape(fracs, 2, TILES, LANES).transpose(0, 2, 1, 3).reshape(-1, LANES)


def shards(
    fields,
    aperture,
    source,
    storage,
    coarse_weight,
    source_slot,
    source_edge,
    destination,
    target_frac,
    target_edge,
    coarse_index,
):
    f32, i32 = jnp.float32, jnp.int32
    fracs = fields.shape[0]
    peers = lax.axis_size(AXES)
    coarse = coarse_weight.shape[0]
    per_dev = coarse // peers
    high = -(-per_dev // LANES)
    columns = lax.axis_size(AXES[1])
    first = lax.axis_index(AXES) * per_dev
    local = coarse_index - first
    none = jnp.zeros_like(local)
    records = jnp.stack(
        [
            destination[:, 0],
            source_slot,
            source_edge,
            target_frac,
            target_edge + 1,
            local >> 7,
            local & (LANES - 1),
            none,
        ],
        0,
    )
    weight = lax.dynamic_slice(coarse_weight, (first,), (per_dev,))
    weight = jnp.pad(weight, (0, 8 * LANES - per_dev)).reshape(8, LANES)
    table = (peers, SLOT)
    sender, target, index = call(
        functools.partial(slots_body, peers, fracs), [(table, i32)] * 3
    )(records)
    arrived = exchange(target)
    groups = fracs // LANES
    turned = (groups, 2 * GRID * GRID, LANES)
    edges_type = ((8 * GRID, fracs), f32)
    cells, sources, openings, edges = call(
        turn_body, [(turned, f32), (turned, f32), ((groups, GRID * GRID, LANES), f32), edges_type]
    )(by_tiles(fields), by_tiles(source), aperture)
    stores = storage.T.reshape(2 * groups, 1, LANES)
    padded = pltpu.VMEM((LANES + 2 * GRID, TILES, LANES), f32)
    block = pltpu.VMEM((LANES, TILES, LANES), f32)
    for step in range(ITERS):
        last = step == ITERS - 1
        rows, mean = call(
            functools.partial(gather_body, peers, fracs),
            [((peers, 2 * GRID, SLOT), f32), (table, f32)],
            [pltpu.VMEM((24 * GRID, fracs), jnp.bfloat16)],
        )(edges, sender)
        rows, extra = call(
            functools.partial(traffic_body, peers, columns, fracs, high),
            [((peers, 2 * GRID, SLOT), f32), ((peers, 8, LANES), f32)],
            [
                pltpu.VMEM((peers, 1, SLOT), f32),
                pltpu.VMEM((peers, 1, SLOT), f32),
                pltpu.VMEM((peers, 8, LANES), f32),
                pltpu.SemaphoreType.DMA((3,)),
                pltpu.SemaphoreType.DMA((3,)),
            ],
            collective_id=0,
            has_side_effects=True,
        )(rows, mean, edges, arrived, index, weight)
        results = call(
            functools.partial(sweep_body, peers, fracs, high, last),
            [((fracs * 2 * TILES, LANES), f32)] if last else [(turned, f32), edges_type],
            [
                pltpu.VMEM((24 * GRID, fracs), f32),
                pltpu.VMEM((16, fracs), f32),
                pltpu.VMEM((groups, 8 * GRID, LANES), f32),
                padded,
                padded,
                padded,
            ]
            + [block] * 5
            + ([pltpu.VMEM(turned, f32)] if last else []),
        )(rows, extra, arrived, edges, cells, openings, sources, stores)
        if last:
            (state,) = results
        else:
            cells, edges = results
    coarse_out = extra.reshape(peers, 8 * LANES)[:, :per_dev].reshape(coarse)
    fields_out = state.reshape(fracs, TILES, 2, LANES).transpose(0, 2, 1, 3).reshape(fields.shape)
    return fields_out, coarse_out


def solution(mesh):
    every = P(AXES)
    return jax.shard_map(
        shards,
        mesh=mesh,
        in_specs=(
            P(AXES, None, None),
            P(AXES, None),
            P(AXES, None, None),
            P(AXES, None),
            P(),
            every,
            every,
            P(AXES, None),
            every,
            every,
            every,
        ),
        out_specs=(P(AXES, None, None), P()),
        check_vma=False,
    )
```
